512 devices in a mesh: lat: 16 (over x, y_hi, core), lon: 32 (over y_lo, z).
Axes of the slice: x: 4, y: 8 (y_hi: 2, y_lo: 4; y = y_hi * 4 + y_lo), z: 8, core: 2. Of those that a mesh axis runs over, the one named last changes fastest.
Arguments:
- tokens: bfloat16 [256, 512, 512], P('lat', 'lon'), may hold values from -6 to 6
- w_qkv0: bfloat16 [8, 192, 512], replicated, may hold values from -4 to 4
- w_out0: bfloat16 [512, 512], replicated, may hold values from -0.25 to 0.25
- gain0: float32 [512], replicated, may hold values from 0.25 to 1.75
- bias0: float32 [8, 225], replicated, may hold values from -4 to 4
- rel0: int32 [64, 64], replicated, may hold values from 0 to 224
- shift: int32 [2], replicated, may hold values from 1 to 7
- gain_merge: float32 [2048], replicated, may hold values from 0.25 to 1.75
- w_merge: bfloat16 [2048, 1024], P('lat'), may hold values from -0.125 to 0.125
- gain1: float32 [1024], replicated, may hold values from 0.25 to 1.75
- w_qkv1: bfloat16 [16, 192, 1024], P('lat'), may hold values from -4 to 4
- w_out1: bfloat16 [1024, 1024], P('lat'), may hold values from -0.1875 to 0.1875
- bias1: float32 [16, 225], P('lat'), may hold values from -4 to 4
- rel1: int32 [64, 64], replicated, may hold values from 0 to 224
Outputs:
- coarse_out: bfloat16 [128, 256, 1024], P('lat', 'lon')
The draws below stay inside these ranges and needn't reach their ends.
All inputs are finite; a program needn't handle non-finite values.
Results may differ from the reference program's by a relative error of at most 0.03.
Values may be sent and summed in bfloat16 or wider, within the bound.
A program may use at most 64 MiB of HBM per device.

```python
import jax
import jax.numpy as jnp
from jax import lax

C0 = 512
HEAD = 64
WIN = 8
C1 = 1024
HEADS0 = 8
HEADS1 = 16
SPAN = 225
H0 = 256
W0 = 512
N_LAT = 16


def head_blocks(key, chans, heads, head):
    normal = jax.random.normal(key, (heads, 3 * head, chans), jnp.float32)
    return jnp.clip(normal, -6.0, 6.0) * chans ** (-0.5)


def draw_w_qkv0(key, part):
    key = jax.random.fold_in(key, 5)
    base = head_blocks(key, C0, HEADS0, HEAD)
    return jnp.clip(base, -4.0, 4.0).astype(jnp.bfloat16)


def draw_w_qkv1(key, part):
    key = jax.random.fold_in(key, 9)
    base = head_blocks(key, C1, HEADS1, HEAD)
    return jnp.clip(base, -4.0, 4.0).astype(jnp.bfloat16)


def place_ends(values, own_key, least, high):
    extent = values.shape
    place = [jax.random.randint(jax.random.fold_in(own_key, axis), (), 0, extent[axis]) for axis in range(len(extent))]
    values = values.at[tuple(place)].set(least)
    longest = extent.index(max(extent))
    place[longest] = (place[longest] + 1) % extent[longest]
    return values.at[tuple(place)].set(high)


def steps_of(rng, shape, pieces, smallest, largest):
    loudness, own = 1.0, jax.random.fold_in(rng, 6)
    for position, parts in pieces:
        steps = jnp.exp(jax.random.uniform(jax.random.fold_in(own, position), (parts,), jnp.float32, smallest / len(pieces), largest / len(pieces)))
        loudness = loudness * jnp.repeat(steps, shape[position] // parts).reshape([-1 if axis == position else 1 for axis in range(len(shape))])
    return loudness


def gaussian(stream_key, dims, scale, bound, shards=(), kind=jnp.bfloat16):
    level = steps_of(stream_key, dims, shards, -0.22, 0.18) if shards else 1.0
    values = jax.random.normal(stream_key, dims, jnp.float32) * scale * level
    return jnp.minimum(jnp.maximum(values, -bound), bound).astype(kind)


def setup_inputs(seed: int = 0) -> dict:
    splits = jax.random.split(jax.random.key(seed), 15)
    tokens = gaussian(splits[0], (H0, W0, C0), 1.0, 6.0, ((0, 16), (1, 32)))
    w_qkv0 = draw_w_qkv0(jax.random.fold_in(splits[14], 71), 0)
    w_out0 = gaussian(splits[2], (C0, C0), C0 ** -0.5, 0.25)
    gain0 = jnp.clip(1.0 + 0.15 * jax.random.normal(splits[3], (C0,), jnp.float32), 0.25, 1.75)
    bias0 = gaussian(splits[4], (HEADS0, SPAN), 1.0, 4.0, (), jnp.float32)
    rel0 = place_ends(jax.random.randint(splits[5], (WIN * WIN, WIN * WIN), 0, SPAN), jax.random.fold_in(splits[5], 1), 0, SPAN - 1).astype(jnp.int32)
    shift = jax.random.randint(splits[6], (2,), 1, WIN).astype(jnp.int32)
    gain_merge = jnp.clip(1.0 + 0.15 * jax.random.normal(splits[7], (4 * C0,), jnp.float32), 0.25, 1.75)
    w_merge = gaussian(splits[8], (4 * C0, C1), (4 * C0) ** -0.5, 0.125, ((0, 16),))
    gain1 = jnp.clip(1.0 + 0.15 * jax.random.normal(splits[9], (C1,), jnp.float32), 0.25, 1.75)
    w_qkv1 = draw_w_qkv1(jax.random.fold_in(splits[14], 71), 0)
    w_out1 = gaussian(splits[11], (C1, C1), C1 ** -0.5, 0.1875, ((0, 16),))
    bias1 = gaussian(splits[12], (HEADS1, SPAN), 1.0, 4.0, ((0, 16),), jnp.float32)
    rel1 = place_ends(jax.random.randint(splits[13], (WIN * WIN, WIN * WIN), 0, SPAN), jax.random.fold_in(splits[13], 1), 0, SPAN - 1).astype(jnp.int32)
    return dict(tokens=tokens, w_qkv0=w_qkv0, w_out0=w_out0, gain0=gain0, bias0=bias0, rel0=rel0, shift=shift, gain_merge=gain_merge, w_merge=w_merge, gain1=gain1, w_qkv1=w_qkv1, w_out1=w_out1, bias1=bias1, rel1=rel1)


EPS = 1e-05
NEG = -1e+30

def stored(values):
    return lax.optimization_barrier(values.astype(jnp.bfloat16))

def layer_norm(values, gain):
    mean = lax.optimization_barrier(jnp.mean(values, axis=-1, keepdims=True))
    centred = values - mean
    spread = lax.optimization_barrier(jnp.mean(centred * centred, axis=-1, keepdims=True))
    return centred * lax.rsqrt(spread + EPS) * gain

def attend(qkv, bias, valid):
    head = qkv.shape[-1] // 3
    wide = qkv.astype(jnp.float32)
    query = wide[..., :head]
    keys = wide[..., head:2 * head]
    values = wide[..., 2 * head:]
    scores = jnp.einsum('wqhd,wkhd->whqk', query, keys) * head ** (-0.5) + bias[None]
    scores = jnp.where(valid[:, None, None, :], scores, NEG)
    peak = lax.optimization_barrier(jnp.max(scores, axis=-1, keepdims=True))
    weights = jnp.exp(scores - peak)
    probs = stored(weights / lax.optimization_barrier(jnp.sum(weights, axis=-1, keepdims=True)))
    mixed = jnp.einsum('whqk,wkhd->wqhd', probs.astype(jnp.float32), values)
    return stored(mixed)

def reference(tokens, w_qkv0, w_out0, gain0, bias0, rel0, shift, gain_merge, w_merge, gain1, w_qkv1, w_out1, bias1, rel1):
    height, width, chans = tokens.shape
    heads0 = w_qkv0.shape[0]
    head = w_qkv0.shape[1] // 3
    size = WIN * WIN
    lat_move = WIN - shift[0]
    lon_move = WIN - shift[1]
    padded = jnp.concatenate([tokens, jnp.zeros((WIN, width, chans), tokens.dtype)], axis=0)
    inside = jnp.arange(height + WIN, dtype=jnp.int32) < height
    padded = jnp.roll(padded, (lat_move, lon_move), axis=(0, 1))
    inside = jnp.roll(inside, lat_move)
    bias_zero = bias0[:, rel0]
    bands = padded.reshape(height // WIN + 1, WIN, width, chans)
    inside_bands = inside.reshape(height // WIN + 1, WIN)
    across = width // WIN
    matrix0 = w_qkv0.reshape(-1, chans).T

    def band_step(pair):
        band, rows_in = pair
        normed = stored(layer_norm(band.astype(jnp.float32), gain0))
        qkv = stored(jnp.dot(normed.reshape(-1, chans), matrix0, preferred_element_type=jnp.float32))
        qkv = qkv.reshape(WIN, across, WIN, heads0, 3 * head).transpose(1, 0, 2, 3, 4).reshape(across, size, heads0, 3 * head)
        valid = jnp.broadcast_to(rows_in[None, :, None], (across, WIN, WIN)).reshape(across, size)
        mixed = attend(qkv, bias_zero, valid)
        return mixed.reshape(across, WIN, WIN, chans).transpose(1, 0, 2, 3).reshape(WIN, width, chans)
    attended = lax.map(band_step, (bands, inside_bands)).reshape(height + WIN, width, chans)
    attended = jnp.roll(attended, (-lat_move, -lon_move), axis=(0, 1))[:height]
    projected = jnp.dot(attended.reshape(-1, chans), w_out0, preferred_element_type=jnp.float32).reshape(height, width, chans)
    fine = stored(tokens.astype(jnp.float32) + projected)
    half_h, half_w = (height // 2, width // 2)
    count = half_h * half_w
    blocks = fine.reshape(half_h, 2, half_w, 2, chans).transpose(0, 2, 1, 3, 4).reshape(count, 4 * chans)
    merged = stored(layer_norm(blocks.astype(jnp.float32), gain_merge))
    coarse_width = w_merge.shape[1]
    share = 4 * chans // N_LAT

    def merge_part(total, index):
        part = lax.dynamic_slice_in_dim(merged, index * share, share, 1)
        rows_w = lax.dynamic_slice_in_dim(w_merge, index * share, share, 0)
        term = stored(jnp.dot(part, rows_w, preferred_element_type=jnp.float32))
        return (total + term.astype(jnp.float32), None)
    summed, _ = lax.scan(merge_part, jnp.zeros((count, coarse_width), jnp.float32), jnp.arange(N_LAT, dtype=jnp.int32))
    coarse = stored(summed)
    normed1 = stored(layer_norm(coarse.astype(jnp.float32), gain1))
    heads1 = w_qkv1.shape[0]
    qkv1 = stored(jnp.dot(normed1, w_qkv1.reshape(-1, coarse_width).T, preferred_element_type=jnp.float32))
    windows = qkv1.reshape(half_h // WIN, WIN, half_w // WIN, WIN, heads1, 3 * head).transpose(0, 2, 1, 3, 4, 5).reshape(-1, size, heads1, 3 * head)
    everyone = jnp.ones((windows.shape[0], size), dtype=bool)
    mixed1 = attend(windows, bias1[:, rel1], everyone)
    attn1 = mixed1.reshape(half_h // WIN, half_w // WIN, WIN, WIN, heads1 * head).transpose(0, 2, 1, 3, 4).reshape(count, heads1 * head)
    head_share = heads1 * head // N_LAT

    def out_part(total, index):
        part = lax.dynamic_slice_in_dim(attn1, index * head_share, head_share, 1)
        rows_w = lax.dynamic_slice_in_dim(w_out1, index * head_share, head_share, 0)
        term = stored(jnp.dot(part, rows_w, preferred_element_type=jnp.float32))
        return (total + term.astype(jnp.float32), None)
    update, _ = lax.scan(out_part, jnp.zeros((count, coarse_width), jnp.float32), jnp.arange(N_LAT, dtype=jnp.int32))
    result = (coarse.astype(jnp.float32) + update).astype(jnp.bfloat16)
    return result.reshape(half_h, half_w, coarse_width)
```

```python
import functools

import jax
import jax.numpy as jnp
from jax import lax
from jax.experimental import pallas as pl
from jax.experimental.pallas import tpu as pltpu
from jax.sharding import PartitionSpec as P

WIN = 8
EPS = 1e-05
NEG = -1e30
MESH = pl.DeviceIdType.MESH
F32 = jnp.float32
BF16 = jnp.bfloat16
PAIR_ORDER = (0, 2, 4, 6, 1, 3, 5, 7)


def place():
    lat = lax.axis_index("lat")
    lon = lax.axis_index("lon")
    x = lax.div(lat, 4)
    half = lax.rem(lax.div(lat, 2), 2)
    core = lax.rem(lat, 2)
    y = half * 4 + lax.div(lon, 8)
    z = lax.rem(lon, 8)
    return lat, lon, x, y, z, core


def at(x, y, z, core):
    return (
        lax.rem(x + 4, 4) * 4 + lax.div(y, 4) * 2 + core,
        lax.rem(y, 4) * 8 + lax.rem(z + 8, 8),
    )


def dot_nt(left, right):
    return lax.dot_general(left, right, (((1,), (1,)), ((), ())), preferred_element_type=F32)


def dot_nn(left, right):
    return jnp.dot(left, right, preferred_element_type=F32)


def norm_rows(values, gain):
    mean = jnp.mean(values, axis=-1, keepdims=True)
    centred = values - mean
    spread = jnp.mean(centred * centred, axis=-1, keepdims=True)
    return centred * lax.rsqrt(spread + EPS) * gain


def lane_masks():
    lane = lax.broadcasted_iota(jnp.int32, (64, 128), 1)
    return lane < 64


def attend_pair(q2, k2, v2, bias, mask):
    low = lane_masks()
    low_b = low.astype(F32).astype(BF16)
    high_b = (1.0 - low.astype(F32)).astype(BF16)
    keys = jnp.concatenate([k2 * low_b, k2 * high_b], axis=0)
    scores = dot_nt(q2, keys) + bias
    if mask is not None:
        scores = scores + mask
    peak_a = jnp.max(jnp.where(low, scores, -jnp.inf), axis=-1, keepdims=True)
    peak_b = jnp.max(jnp.where(low, -jnp.inf, scores), axis=-1, keepdims=True)
    weights = jnp.exp(scores - jnp.where(low, peak_a, peak_b)).astype(BF16)
    values = jnp.concatenate([v2 * low_b, v2 * high_b], axis=0)
    ones = jnp.concatenate([low_b, high_b], axis=0)
    mixed = dot_nn(weights, jnp.concatenate([values, ones], axis=1))
    return (mixed[:, :128] / mixed[:, 128:]).astype(BF16)


def fill_bias(table, rel2, out):
    coarse_part = table.astype(BF16).astype(F32)
    split = jnp.concatenate([coarse_part, table - coarse_part], axis=0).astype(BF16)
    entry = lax.broadcasted_iota(jnp.int32, (256, 128), 0)
    low = lax.broadcasted_iota(jnp.int32, (4, 128), 1) < 64

    def step(p, carry):
        row = rel2[pl.ds(p, 1), :]
        onehot = jnp.where(entry == row, 1.0, 0.0).astype(BF16)
        both = dot_nn(split, onehot)
        both = both[:8] + both[8:]
        packed = jnp.where(low, both[:4], both[4:])
        for t in range(4):
            out[t, pl.ds(p, 1), :] = packed[t : t + 1]
        return carry

    lax.fori_loop(0, 64, step, 0, unroll=4)


def kernel(
    shift, tok, w0, wo0, g0, rel0, tab0, gm, wm, g1, wq, wo, tab1, rel1,
    out,
    fine_ref, hq, wide_m, wide_q, wide_o, tabs, b0, b1, mg, mo,
    part_s, part_r, both, upd_s, upd_r, coarse_ref, attn, ss, rs, ls,
):
    lat, lon, x, y, z, core = place()
    half = lax.div(y, 4)
    a = shift[0]
    b = shift[1]

    here = (x, y, z, core)
    to_xp, to_xm, to_x2 = at(x + 1, y, z, core), at(x - 1, y, z, core), at(x + 2, y, z, core)
    to_mir = at(x, 7 - y, z, core)
    to_zp, to_zm = at(x, y, z + 1, core), at(x, y, z - 1, core)
    to_core = at(x, y, z, 1 - core)
    up, down = lax.rem(lat + 15, 16), lax.rem(lat + 1, 16)
    left, right = lax.rem(lon + 31, 32), lax.rem(lon + 1, 32)

    barrier = pltpu.get_barrier_semaphore()
    partners = [
        to_xp, to_xm, to_x2, to_mir, to_zp, to_zm, to_core,
        (up, lon), (down, lon), (lat, left), (lat, right),
        (up, left), (up, right), (down, left), (down, right),
    ]
    for dev in partners:
        pl.semaphore_signal(barrier, inc=1, device_id=dev, device_id_type=MESH)
    pl.semaphore_wait(barrier, len(partners))

    made = []

    def remote(src, dst, dev):
        k = len(made)
        copy = pltpu.make_async_remote_copy(
            src_ref=src, dst_ref=dst, send_sem=ss.at[k], recv_sem=rs.at[k],
            device_id=dev, device_id_type=MESH,
        )
        made.append(copy)
        return copy

    halo_lon = [
        remote(tok.at[1], hq.at[4], (lat, right)),
        remote(tok.at[3], hq.at[8], (lat, right)),
        remote(tok.at[0], hq.at[7], (lat, left)),
        remote(tok.at[2], hq.at[11], (lat, left)),
    ]
    halo_lat = [
        remote(tok.at[pl.ds(2, 2)], hq.at[pl.ds(1, 2)], (down, lon)),
        remote(tok.at[pl.ds(0, 2)], hq.at[pl.ds(13, 2)], (up, lon)),
        remote(tok.at[3], hq.at[0], (down, right)),
        remote(tok.at[2], hq.at[3], (down, left)),
        remote(tok.at[1], hq.at[12], (up, right)),
        remote(tok.at[0], hq.at[15], (up, left)),
    ]
    for copy in halo_lat + halo_lon:
        copy.start()

    parity = lax.rem(z, 2)
    pieces = [(wm, wide_m, 128), (wq, wide_q, 192), (wo, wide_o, 64)]
    first, second, share_a, share_b, locals_ = [], [], [], [], []
    tab_first = [
        remote(tab1, tabs.at[2], to_xp),
        remote(tab1, tabs.at[1], to_xm),
        remote(tab1, tabs.at[3], to_x2),
        remote(tab1, tabs.at[4], to_mir),
    ]
    tab_second = [
        remote(tabs.at[4], tabs.at[6], to_xp),
        remote(tabs.at[4], tabs.at[5], to_xm),
        remote(tabs.at[4], tabs.at[7], to_x2),
    ]
    for n, (src, wide, rows) in enumerate(pieces):
        size = rows // 2
        start = pl.multiple_of(parity * size, 16)
        mine = pl.ds(start, size)
        quarter_a = pl.ds(start, size // 2)
        quarter_b = pl.ds(pl.multiple_of(start + size // 2, 16), size // 2)
        first.append([
            remote(src.at[mine], wide.at[2, mine], to_xp),
            remote(src.at[mine], wide.at[1, mine], to_xm),
            remote(src.at[mine], wide.at[3, mine], to_x2),
            remote(src.at[mine], wide.at[4, mine], to_mir),
        ])
        far = (
            remote(wide.at[4, mine], wide.at[7, mine], to_x2)
            if n == 1
            else remote(wide.at[3, mine], wide.at[7, mine], to_mir)
        )
        second.append([
            remote(wide.at[4, mine], wide.at[6, mine], to_xp),
            remote(wide.at[4, mine], wide.at[5, mine], to_xm),
            far,
        ])
        share_a.append([
            remote(wide.at[pl.ds(1, 4), quarter_a], wide.at[pl.ds(1, 4), quarter_a], to_zp),
            remote(wide.at[pl.ds(1, 4), quarter_b], wide.at[pl.ds(1, 4), quarter_b], to_zm),
        ])
        share_b.append([
            remote(wide.at[pl.ds(5, 3), quarter_a], wide.at[pl.ds(5, 3), quarter_a], to_zp),
            remote(wide.at[pl.ds(5, 3), quarter_b], wide.at[pl.ds(5, 3), quarter_b], to_zm),
        ])
        locals_.append(pltpu.make_async_copy(src, wide.at[0], ls.at[n]))
    locals_.append(pltpu.make_async_copy(tab1, tabs.at[0], ls.at[3]))

    def start_all(copies):
        for copy in copies:
            copy.start()

    def recv_all(copies):
        for copy in copies:
            copy.wait_recv()

    start_all(tab_first)
    for n in range(3):
        start_all(first[n])
    start_all(locals_)

    def stage_two(n):
        recv_all(first[n])
        start_all(second[n])
        start_all(share_a[n])

    def stage_three(n):
        recv_all(second[n])
        start_all(share_b[n])

    for i in range(2):
        for j in range(2):
            hq[4 * i + j + 5] = tok[2 * i + j]
    want = lax.broadcasted_iota(jnp.int32, (192, 1), 0)
    want_r = a + ((want & 63) >> 3)
    want_c = b + 8 * (want >> 6) + (want & 7)
    want = (want_r >> 3) * 256 + (want_c >> 3) * 64 + (want_r & 7) * 8 + (want_c & 7)
    pick = lax.broadcasted_iota(jnp.int32, (192, 512), 1) == want
    pick = jnp.where(pick, 1.0, 0.0).astype(BF16)
    fill_bias(tab0[...], rel0, b0)

    def window_row(k, carry):
        i = lax.rem(k + 1, 3)

        @pl.when(k == 0)
        def _():
            recv_all(halo_lon)

        @pl.when(k == 1)
        def _():
            stage_two(0)
            recv_all(halo_lat)

        @pl.when(k == 2)
        def _():
            stage_two(1)
            stage_three(0)

        cells = dot_nn(pick, hq[pl.ds(4 * i, 8)].reshape(512, 512))
        normed = norm_rows(cells, g0[...]).astype(BF16)
        query = (dot_nt(normed, w0[:, 0:64, :].reshape(512, 512)) * 0.125).astype(BF16)
        keys = dot_nt(normed, w0[:, 64:128, :].reshape(512, 512)).astype(BF16)
        values = dot_nt(normed, w0[:, 128:192, :].reshape(512, 512)).astype(BF16)
        lane = lax.broadcasted_iota(jnp.int32, (1, 128), 1)
        row = lat * 16 + a - 8 + 8 * i + ((lane & 63) >> 3)
        mask = jnp.where((row >= 0) & (row < 256), 0.0, NEG)
        for w in range(3):
            rows = slice(64 * w, 64 * w + 64)
            for t in range(4):
                cols = slice(128 * t, 128 * t + 128)
                attn[rows, cols] = attend_pair(
                    query[rows, cols], keys[rows, cols], values[rows, cols], b0[t], mask
                )
        fine = cells + dot_nn(attn[...], wo0[...])
        fine_ref[pl.ds(pl.multiple_of(192 * i, 64), 192), :] = fine.astype(BF16)
        return carry

    lax.fori_loop(0, 3, window_row, 0)
    stage_two(2)
    stage_three(1)
    recv_all(tab_first)
    start_all(tab_second)

    want = lax.broadcasted_iota(jnp.int32, (256, 1), 0)
    want_r = 8 - a + 2 * ((want >> 3) & 7) + (want >> 7)
    want_c = 8 - b + 2 * (want & 7) + ((want >> 6) & 1)
    want = (want_r >> 3) * 192 + (want_c >> 3) * 64 + (want_r & 7) * 8 + (want_c & 7)
    pick = lax.broadcasted_iota(jnp.int32, (256, 576), 1) == want
    pick = jnp.where(pick, 1.0, 0.0).astype(BF16)
    picked = dot_nn(pick, fine_ref[...])
    blocks = [picked[64 * k : 64 * k + 64] for k in range(4)]
    total = sum(jnp.sum(block, axis=-1, keepdims=True) for block in blocks)
    mean = total * (1.0 / 2048)
    blocks = [block - mean for block in blocks]
    spread = sum(jnp.sum(block * block, axis=-1, keepdims=True) for block in blocks)
    scale = lax.rsqrt(spread * (1.0 / 2048) + EPS)
    for k in range(4):
        merged = (blocks[k] * scale * gm[:, 512 * k : 512 * k + 512]).astype(BF16)
        for m in range(4):
            chunk = 4 * k + m
            mg[chunk % 2, chunk // 2] = merged[:, 128 * m : 128 * m + 128]

    give_merged = remote(mg.at[1 - core], mo, to_core)
    give_part = remote(part_s, part_r, to_core)
    give_norm = remote(both.at[0], both.at[1], to_core)
    give_upd = remote(upd_s, upd_r, to_core)
    give_merged.start()
    stage_three(2)
    recv_all(tab_second)
    for copy in locals_:
        copy.wait()
    sub = lax.broadcasted_iota(jnp.int32, (8, 256), 0)
    table = jnp.zeros((8, 256), F32)
    for n, slot in enumerate(PAIR_ORDER):
        table = jnp.where(sub == n, tabs[slot], table)
    fill_bias(table, rel1, b1)

    recv_all(share_a[0])
    recv_all(share_b[0])
    give_merged.wait_recv()
    slots = [
        2 * lax.rem(x + step, 4) + side for side in (half, 1 - half) for step in (0, 1, 3, 2)
    ]
    mine = jnp.concatenate([mg[core, slot] for slot in slots], axis=1)
    theirs = jnp.concatenate([mo[slot] for slot in slots], axis=1)
    merged = jnp.concatenate([theirs, mine], axis=0)
    partial = dot_nn(merged, wide_m[...].reshape(1024, 1024))
    part_s[...] = partial[:64].astype(BF16)
    give_part.start()
    give_part.wait_recv()
    coarse = (partial[64:] + part_r[...].astype(F32)).astype(BF16)
    coarse_ref[...] = coarse
    both[0] = norm_rows(coarse.astype(F32), g1[...]).astype(BF16)
    give_norm.start()
    recv_all(share_a[1])
    recv_all(share_b[1])
    give_norm.wait_recv()
    normed = both[...].reshape(128, 1024)
    query = (dot_nt(normed, wide_q[:, 0:64, :].reshape(512, 1024)) * 0.125).astype(BF16)
    keys = dot_nt(normed, wide_q[:, 64:128, :].reshape(512, 1024)).astype(BF16)
    values = dot_nt(normed, wide_q[:, 128:192, :].reshape(512, 1024)).astype(BF16)
    for w in range(2):
        rows = slice(64 * w, 64 * w + 64)
        for t in range(4):
            cols = slice(128 * t, 128 * t + 128)
            attn[rows, cols] = attend_pair(
                query[rows, cols], keys[rows, cols], values[rows, cols], b1[t], None
            )
    recv_all(share_a[2])
    recv_all(share_b[2])
    update = dot_nn(attn[0:128, :], wide_o[...].reshape(512, 1024))
    upd_s[...] = update[64:].astype(BF16)
    give_upd.start()
    give_upd.wait_recv()
    out[...] = (coarse_ref[...].astype(F32) + update[:64] + upd_r[...].astype(F32)).astype(BF16)
    for copy in made:
        copy.wait_send()


COPIES = 10 + 7 + 3 * 11 + 4


def on_device(
    tokens, w_qkv0, w_out0, gain0, bias0, rel0, shift, gain_merge, w_merge, gain1, w_qkv1,
    w_out1, bias1, rel1,
):
    tok = tokens.reshape(2, 8, 2, 8, 512).transpose(0, 2, 1, 3, 4).reshape(4, 64, 512)
    tab0 = jnp.pad(bias0, ((0, 0), (0, 31)))
    tab0 = jnp.concatenate([tab0[0::2], tab0[1::2]], axis=0)
    tab1 = jnp.broadcast_to(jnp.pad(bias1, ((0, 0), (0, 31))), (8, 256))
    twice0 = jnp.concatenate([rel0, rel0], axis=1)
    twice1 = jnp.concatenate([rel1, rel1], axis=1)
    vmem = pl.BlockSpec(memory_space=pltpu.VMEM)
    smem = pl.BlockSpec(memory_space=pltpu.SMEM)
    result = pl.pallas_call(
        kernel,
        out_shape=jax.ShapeDtypeStruct((64, 1024), BF16),
        in_specs=[smem] + [vmem] * 13,
        out_specs=vmem,
        scratch_shapes=[
            pltpu.VMEM((576, 512), BF16),
            pltpu.VMEM((16, 64, 512), BF16),
            pltpu.VMEM((8, 128, 1024), BF16),
            pltpu.VMEM((8, 192, 1024), BF16),
            pltpu.VMEM((8, 64, 1024), BF16),
            pltpu.VMEM((8, 8, 256), F32),
            pltpu.VMEM((4, 64, 128), F32),
            pltpu.VMEM((4, 64, 128), F32),
            pltpu.VMEM((2, 8, 64, 128), BF16),
            pltpu.VMEM((8, 64, 128), BF16),
            pltpu.VMEM((64, 1024), BF16),
            pltpu.VMEM((64, 1024), BF16),
            pltpu.VMEM((2, 64, 1024), BF16),
            pltpu.VMEM((64, 1024), BF16),
            pltpu.VMEM((64, 1024), BF16),
            pltpu.VMEM((64, 1024), BF16),
            pltpu.VMEM((192, 512), BF16),
            pltpu.SemaphoreType.DMA((COPIES,)),
            pltpu.SemaphoreType.DMA((COPIES,)),
            pltpu.SemaphoreType.DMA((4,)),
        ],
        compiler_params=pltpu.CompilerParams(
            collective_id=0, has_side_effects=True, vmem_limit_bytes=48 << 20
        ),
        name="swin",
    )(
        shift, tok, w_qkv0, w_out0, gain0.reshape(1, 512), twice0, tab0,
        gain_merge.reshape(1, 2048), w_merge, gain1.reshape(1, 1024),
        w_qkv1.reshape(192, 1024), w_out1, tab1, twice1,
    )
    return result.reshape(8, 8, 1024)


def solution(mesh):
    placed = (
        P("lat", "lon", None),
        P(),
        P(),
        P(),
        P(),
        P(),
        P(),
        P(),
        P("lat", None),
        P(),
        P("lat", None, None),
        P("lat", None),
        P("lat", None),
        P(),
    )
    return jax.shard_map(
        on_device, mesh=mesh, in_specs=placed, out_specs=P("lat", "lon", None), check_vma=False
    )
```

```python
import functools

import jax
import jax.numpy as jnp
from jax import lax
from jax.experimental import pallas as pl
from jax.experimental.pallas import tpu as pltpu
from jax.sharding import PartitionSpec as P

WIN = 8
EPS = 1e-05
NEG = -1e30
MESH = pl.DeviceIdType.MESH
F32 = jnp.float32
BF16 = jnp.bfloat16


def place():
    lat = lax.axis_index("lat")
    lon = lax.axis_index("lon")
    x = lax.div(lat, 4)
    half = lax.rem(lax.div(lat, 2), 2)
    core = lax.rem(lat, 2)
    y = half * 4 + lax.div(lon, 8)
    z = lax.rem(lon, 8)
    return lat, lon, x, y, z, core


def at(x, y, z, core):
    return (
        lax.rem(x + 4, 4) * 4 + lax.div(y, 4) * 2 + core,
        lax.rem(y, 4) * 8 + lax.rem(z + 8, 8),
    )


def dot_nt(left, right):
    return lax.dot_general(left, right, (((1,), (1,)), ((), ())), preferred_element_type=F32)


def dot_nn(left, right):
    return jnp.dot(left, right, preferred_element_type=F32)


def norm_rows(values, gain):
    mean = jnp.mean(values, axis=-1, keepdims=True)
    centred = values - mean
    spread = jnp.mean(centred * centred, axis=-1, keepdims=True)
    return centred * lax.rsqrt(spread + EPS) * gain


def lane_masks():
    lane = lax.broadcasted_iota(jnp.int32, (64, 128), 1)
    return lane < 64


def attend_pair(q2, k2, v2, bias, mask):
    low = lane_masks()
    low_b = low.astype(F32).astype(BF16)
    high_b = (1.0 - low.astype(F32)).astype(BF16)
    keys = jnp.concatenate([k2 * low_b, k2 * high_b], axis=0)
    scores = dot_nt(q2, keys) + bias
    if mask is not None:
        scores = scores + mask
    peak_a = jnp.max(jnp.where(low, scores, -jnp.inf), axis=-1, keepdims=True)
    peak_b = jnp.max(jnp.where(low, -jnp.inf, scores), axis=-1, keepdims=True)
    weights = jnp.exp(scores - jnp.where(low, peak_a, peak_b)).astype(BF16)
    values = jnp.concatenate([v2 * low_b, v2 * high_b], axis=0)
    ones = jnp.concatenate([low_b, high_b], axis=0)
    mixed = dot_nn(weights, jnp.concatenate([values, ones], axis=1))
    return (mixed[:, :128] / mixed[:, 128:]).astype(BF16)


def fill_bias(table, rel, rel2, out):
    coarse_part = table.astype(BF16).astype(F32)
    split = jnp.concatenate([coarse_part, table - coarse_part], axis=0).astype(BF16)
    entry = lax.broadcasted_iota(jnp.int32, (256, 256), 0)
    low = lax.broadcasted_iota(jnp.int32, (1, 128), 1) < 64
    rel2[...] = jnp.concatenate([rel[:32], rel[:32], rel[32:], rel[32:]], axis=1)

    def step(p, carry):
        row = rel2[pl.ds(p, 1), :]
        onehot = jnp.where(entry == row, 1.0, 0.0).astype(BF16)
        found = dot_nn(split, onehot)
        found = found[:8] + found[8:]
        for side in range(2):
            cols = slice(128 * side, 128 * side + 128)
            for t in range(4):
                out[t, pl.ds(p + 32 * side, 1), :] = jnp.where(
                    low, found[2 * t : 2 * t + 1, cols], found[2 * t + 1 : 2 * t + 2, cols]
                )
        return carry

    lax.fori_loop(0, 32, step, 0, unroll=4)


def kernel(
    shift, tok_h, w0_h, wo0_h, g0_h, rel0_h, bias0_h, gm_h, wm, g1_h, wq, wo, bias1_h, rel1_h,
    out,
    tok, w0, wo0, g0, rel0, bias0, gm, g1, bias1, rel1, tab0, rel2,
    fine_ref, hq, wide_m, wide_q, wide_o, tabs, b0, b1, mg, mo,
    part_s, part_r, upd_s, upd_r, coarse_ref, attn, ss, rs, ls,
):
    loads = [
        pltpu.make_async_copy(src, dst, ls.at[n])
        for n, (src, dst) in enumerate([
            (tok_h, tok), (bias1_h, bias1), (bias0_h, bias0), (rel0_h, rel0), (g0_h, g0),
            (w0_h, w0), (wo0_h, wo0), (gm_h, gm), (g1_h, g1), (rel1_h, rel1),
            (wm, wide_m.at[0]), (wq, wide_q.at[0]), (wo, wide_o.at[0]),
        ])
    ]
    for copy in loads:
        copy.start()
    lat, lon, x, y, z, core = place()
    half = lax.div(y, 4)
    a = shift[0]
    b = shift[1]

    to_xp, to_xm, to_x2 = at(x + 1, y, z, core), at(x - 1, y, z, core), at(x + 2, y, z, core)
    to_mir = at(x, 7 - y, z, core)
    to_yp, to_ym = at(x, lax.rem(y + 1, 8), z, core), at(x, lax.rem(y + 7, 8), z, core)
    to_zp, to_zm = at(x, y, z + 1, core), at(x, y, z - 1, core)
    to_core = at(x, y, z, 1 - core)
    to_pair = at(x, y + 1 - 2 * lax.rem(y, 2), z, core)
    depth = lax.rem(y, 4)
    edge = (depth == 0) | (depth == 3)
    outward = jnp.where(depth < 2, 7, 1)
    to_out = at(x, lax.rem(y + outward, 8), z, core)
    to_in = at(x, lax.rem(y + 8 - outward, 8), z, core)
    to_out2 = at(x, lax.rem(y + 2 * outward, 8), z, core)
    to_y2, to_ym2 = at(x, lax.rem(y + 2, 8), z, core), at(x, lax.rem(y + 6, 8), z, core)
    near, far = lax.rem(lat + 1 + 14 * core, 16), lax.rem(lat + 15 + 2 * core, 16)
    left, right = lax.rem(lon + 31, 32), lax.rem(lon + 1, 32)

    barrier = pltpu.get_barrier_semaphore()
    partners = [
        to_xp, to_xm, to_x2, to_mir, to_yp, to_ym, to_zp, to_zm, to_core,
        (far, lon), (lat, left), (lat, right), to_y2, to_ym2,
    ]
    for dev in partners:
        pl.semaphore_signal(barrier, inc=1, device_id=dev, device_id_type=MESH)
    loads[0].wait()
    for i in range(2):
        for j in range(2):
            block = tok[8 * i : 8 * i + 8].astype(F32)[:, 8 * j : 8 * j + 8, :]
            hq[4 * i + j + 5] = block.reshape(64, 512).astype(BF16)
    loads[1].wait()
    tabs[0] = jnp.zeros((8, 256), F32)
    tabs[0, :, 0:225] = jnp.broadcast_to(bias1[...], (8, 225))
    pl.semaphore_wait(barrier, len(partners))

    made = []

    def remote(src, dst, dev, take=None):
        k = len(made)
        copy = pltpu.make_async_remote_copy(
            src_ref=src, dst_ref=dst, send_sem=ss.at[k],
            recv_sem=rs.at[k if take is None else take],
            device_id=dev, device_id_type=MESH,
        )
        made.append(copy)
        return copy

    def start_all(copies):
        for copy in copies:
            copy.start()

    def recv_all(copies):
        for copy in copies:
            copy.wait_recv()

    far_at = 1 + 12 * core
    halo_near = [remote(hq.at[pl.ds(9 - 4 * core, 2)], hq.at[pl.ds(1 + 12 * core, 2)], (near, lon))]
    halo_far = [remote(hq.at[pl.ds(5 + 4 * core, 2)], hq.at[pl.ds(13 - 12 * core, 2)], (far, lon))]
    halo_lon = [
        remote(hq.at[6], hq.at[4], (lat, right)),
        remote(hq.at[10], hq.at[8], (lat, right)),
        remote(hq.at[5], hq.at[7], (lat, left)),
        remote(hq.at[9], hq.at[11], (lat, left)),
    ]
    corner_near = [
        remote(hq.at[8 - 4 * core], hq.at[12 * core], (near, lon)),
        remote(hq.at[11 - 4 * core], hq.at[3 + 12 * core], (near, lon)),
    ]
    corner_far = [
        remote(hq.at[far_at + 1], hq.at[far_at - 1], (lat, right)),
        remote(hq.at[far_at], hq.at[far_at + 2], (lat, left)),
    ]
    start_all(halo_lon + halo_near + halo_far)

    parity = lax.rem(z, 2)
    tab_first = [
        remote(tabs.at[0], tabs.at[2], to_xp),
        remote(tabs.at[0], tabs.at[1], to_xm),
        remote(tabs.at[0], tabs.at[3], to_x2),
        remote(tabs.at[0], tabs.at[4], to_mir),
    ]
    tab_second = [
        remote(tabs.at[4], tabs.at[6], to_xp),
        remote(tabs.at[4], tabs.at[5], to_xm),
        remote(tabs.at[4], tabs.at[7], to_x2),
    ]

    class Piece:
        def __init__(self, src, wide, base, rows, name):
            whole, by_y, direct = name in WHOLE, name in BY_Y, name in DIRECT
            size = rows // 2

            def parts(by):
                start = pl.multiple_of(base + by * size, 16)
                return (
                    pl.ds(start, size),
                    pl.ds(start, size // 2),
                    pl.ds(pl.multiple_of(start + size // 2, 16), size // 2),
                )

            part, part_a, part_b = parts(parity)
            side, side_a, side_b = parts(lax.rem(depth, 2) if by_y else parity)
            first = pl.ds(base, rows) if whole else side

            def swap(slot, count):
                slots = pl.ds(slot, count)
                return [
                    remote(wide.at[slots, part_a], wide.at[slots, part_a], to_zp),
                    remote(wide.at[slots, part_b], wide.at[slots, part_b], to_zm),
                ]

            def swap_y(slot, count):
                slots = pl.ds(slot, count)
                return [remote(wide.at[slots, side], wide.at[slots, side], to_pair)]

            self.whole = whole
            self.side = [
                remote(src.at[first], wide.at[2, first], to_xp),
                remote(src.at[first], wide.at[1, first], to_xm),
            ]
            take = len(made)
            self.cross = remote(src.at[part], wide.at[4, part], to_out)
            self.direct = direct
            if direct:
                self.inward = remote(src.at[part], wide.at[4, part], to_out2, take)
            else:
                self.inward = remote(wide.at[4, part], wide.at[4, part], to_in, take)
            self.on = [
                remote(wide.at[2, side_a], wide.at[3, side_a], to_xp),
                remote(wide.at[1, side_b], wide.at[3, side_b], to_xm),
            ]
            self.far_side = [
                remote(wide.at[4, part], wide.at[6, part], to_xp),
                remote(wide.at[4, part], wide.at[5, part], to_xm),
            ]
            self.far_on = [
                remote(wide.at[6, part_a], wide.at[7, part_a], to_xp),
                remote(wide.at[5, part_b], wide.at[7, part_b], to_xm),
            ]
            if by_y:
                self.swaps = [[] if whole else swap_y(1, 2), swap_y(3, 1), swap(4, 3), swap(7, 1)]
            else:
                self.swaps = [[] if whole else swap(1, 2), swap(3, 2), swap(5, 2), swap(7, 1)]

        def step(self, n):
            if n == 0:
                start_all(self.side)
                pl.when(edge)(self.cross.start)
                if self.direct:
                    pl.when(edge)(self.inward.start)
            if n == 1:
                recv_all(self.side)
                start_all(self.on)
                start_all(self.swaps[0])
            if n == 2:
                self.cross.wait_recv()
                if not self.direct:
                    pl.when(edge)(self.inward.start)
                start_all(self.far_side)
            if n == 3:
                recv_all(self.on)
                start_all(self.swaps[1])
            if n == 4:
                recv_all(self.far_side)
                start_all(self.far_on)
                start_all(self.swaps[2])
            if n == 5:
                recv_all(self.far_on)
                start_all(self.swaps[3])

        def finish(self, near):
            for swap in self.swaps[:2] if near else self.swaps[2:]:
                recv_all(swap)

        def sent(self):
            @pl.when(edge)
            def _():
                self.cross.wait_send()
                self.inward.wait_send()

    pieces = {
        "M": Piece(wm, wide_m, 0, 128, "M"),
        "A": Piece(wq, wide_q, 0, 128, "A"),
        "B": Piece(wq, wide_q, 128, 64, "B"),
        "W": Piece(wo, wide_o, 0, 64, "W"),
    }

    def events(name):
        for event in EVENTS[name]:
            if event == "T1":
                start_all(tab_first)
            elif event == "T2":
                recv_all(tab_first)
                start_all(tab_second)
            elif event == "CF":
                recv_all(halo_far)
                start_all(corner_far)
            else:
                pieces[event[1]].step(int(event[0]))

    events("B0")

    want = lax.broadcasted_iota(jnp.int32, (192, 1), 0)
    want_r = a + ((want & 63) >> 3)
    want_c = b + 8 * (want >> 6) + (want & 7)
    want = (want_r >> 3) * 256 + (want_c >> 3) * 64 + (want_r & 7) * 8 + (want_c & 7)
    pick = lax.broadcasted_iota(jnp.int32, (192, 512), 1) == want
    pick = jnp.where(pick, 1.0, 0.0).astype(BF16)
    for copy in loads[2:]:
        copy.wait()
    tab0[...] = jnp.zeros((8, 256), F32)
    tab0[:, 0:225] = bias0[...]
    fill_bias(tab0[...], rel0[...], rel2, b0)

    def window_row(k, carry):
        i = jnp.where(k == 0, 1, jnp.where(k == 1, 2 - 2 * core, 2 * core))

        @pl.when(k == 0)
        def _():
            events("R0a")
            recv_all(halo_lon)
            start_all(corner_near)

        @pl.when(k == 1)
        def _():
            events("R1a")
            recv_all(halo_near)
            recv_all(corner_near)

        @pl.when(k == 2)
        def _():
            events("R2a")
            recv_all(corner_far)

        cells = dot_nn(pick, hq[pl.ds(4 * i, 8)].reshape(512, 512))
        normed = norm_rows(cells, g0[...]).astype(BF16)
        query = (dot_nt(normed, w0[:, 0:64, :].reshape(512, 512)) * 0.125).astype(BF16)
        keys = dot_nt(normed, w0[:, 64:128, :].reshape(512, 512)).astype(BF16)
        values = dot_nt(normed, w0[:, 128:192, :].reshape(512, 512)).astype(BF16)
        for n in range(3):
            pl.when(k == n)(functools.partial(events, "R%db" % n))
        lane = lax.broadcasted_iota(jnp.int32, (1, 128), 1)
        row = lat * 16 + a - 8 + 8 * i + ((lane & 63) >> 3)
        mask = jnp.where((row >= 0) & (row < 256), 0.0, NEG)
        for w in range(3):
            rows = slice(64 * w, 64 * w + 64)
            for t in range(4):
                cols = slice(128 * t, 128 * t + 128)
                attn[rows, cols] = attend_pair(
                    query[rows, cols], keys[rows, cols], values[rows, cols], b0[t], mask
                )
        fine = cells + dot_nn(attn[...], wo0[...])
        fine_ref[pl.ds(pl.multiple_of(192 * i, 64), 192), :] = fine.astype(BF16)
        return carry

    lax.fori_loop(0, 3, window_row, 0)
    events("MG")

    want = lax.broadcasted_iota(jnp.int32, (256, 1), 0)
    want_r = 8 - a + 2 * ((want >> 3) & 7) + (want >> 7)
    want_c = 8 - b + 2 * (want & 7) + ((want >> 6) & 1)
    want = (want_r >> 3) * 192 + (want_c >> 3) * 64 + (want_r & 7) * 8 + (want_c & 7)
    pick = lax.broadcasted_iota(jnp.int32, (256, 576), 1) == want
    pick = jnp.where(pick, 1.0, 0.0).astype(BF16)
    picked = dot_nn(pick, fine_ref[...])
    blocks = [picked[64 * k : 64 * k + 64] for k in range(4)]
    total = sum(jnp.sum(block, axis=-1, keepdims=True) for block in blocks)
    mean = total * (1.0 / 2048)
    blocks = [block - mean for block in blocks]
    spread = sum(jnp.sum(block * block, axis=-1, keepdims=True) for block in blocks)
    scale = lax.rsqrt(spread * (1.0 / 2048) + EPS)
    for k in range(4):
        merged = (blocks[k] * scale * gm[:, 512 * k : 512 * k + 512]).astype(BF16)
        for m in range(4):
            chunk = 4 * k + m
            mg[chunk % 2, chunk // 2] = merged[:, 128 * m : 128 * m + 128]

    give_merged = remote(mg.at[1 - core], mo, to_core)
    give_part = remote(part_s, part_r, to_core)
    give_upd = remote(upd_s, upd_r, to_core)
    give_merged.start()
    events("B1")
    recv_all(tab_second)
    sub = lax.broadcasted_iota(jnp.int32, (8, 256), 0)
    table = jnp.zeros((8, 256), F32)
    for n, slot in enumerate(range(8)):
        table = jnp.where(sub == n, tabs[slot], table)
    fill_bias(table, rel1[...], rel2, b1)

    give_merged.wait_recv()
    slots = [
        2 * lax.rem(x + step, 4) + side for side in (half, 1 - half) for step in (0, 1, 3, 2)
    ]
    mine = jnp.concatenate([mg[core, slot] for slot in slots], axis=1)
    theirs = jnp.concatenate([mo[slot] for slot in slots], axis=1)
    merged = jnp.concatenate([theirs, mine], axis=0)
    events("MM")
    pieces["M"].finish(True)
    partial = dot_nn(merged[:, :512], wide_m[0:4].reshape(512, 1024))
    events("MF")
    pieces["M"].finish(False)
    partial = partial + dot_nn(merged[:, 512:], wide_m[4:8].reshape(512, 1024))
    part_s[...] = partial.astype(BF16)
    give_part.start()
    events("LN")
    give_part.wait_recv()
    coarse = (partial[64:] + part_r[0:64].astype(F32)).astype(BF16)
    coarse_ref[...] = coarse
    others = (partial[:64] + part_r[64:128].astype(F32)).astype(BF16)
    both = jnp.concatenate([coarse, others], axis=0).astype(F32)
    normed = norm_rows(both, g1[...]).astype(BF16)
    for g in range(2):
        events("QN" if g == 0 else "QF")
        pieces["A"].finish(g == 0)
        pieces["B"].finish(g == 0)
        heads = slice(4 * g, 4 * g + 4)
        query = dot_nt(normed, wide_q[heads, 0:64, :].reshape(256, 1024)) * 0.125
        query = query.astype(BF16)
        keys = dot_nt(normed, wide_q[heads, 64:128, :].reshape(256, 1024)).astype(BF16)
        values = dot_nt(normed, wide_q[heads, 128:192, :].reshape(256, 1024)).astype(BF16)
        for w in range(2):
            rows = slice(64 * w, 64 * w + 64)
            for t in range(2):
                cols = slice(128 * t, 128 * t + 128)
                pair = 2 * g + t
                attn[rows, 128 * pair : 128 * pair + 128] = attend_pair(
                    query[rows, cols], keys[rows, cols], values[rows, cols], b1[pair], None
                )
    events("WO")
    pieces["W"].finish(True)
    pieces["W"].finish(False)
    update = dot_nn(attn[0:128, :], wide_o[...].reshape(512, 1024))
    upd_s[...] = update[64:].astype(BF16)
    give_upd.start()
    give_upd.wait_recv()
    out[...] = (coarse_ref[...].astype(F32) + update[:64] + upd_r[...].astype(F32)).astype(BF16)
    for piece in pieces.values():
        piece.sent()
    conditional = [c for piece in pieces.values() for c in (piece.cross, piece.inward)]
    for copy in made:
        if not any(copy is c for c in conditional):
            copy.wait_send()


COPIES = 10 + 7 + 4 * 18 + 3
WHOLE = ""
BY_Y = "BW"
DIRECT = "ABMW"
EVENTS = {
    "B0": ("T1", "0M",),
    "R0a": ("0A",),
    "R0b": ("1A", "1M",),
    "R1a": ("0B", "0W",),
    "R1b": ("CF", "2M", "3M",),
    "R2a": ("1B", "4M",),
    "R2b": ("2A", "3B", "3A",),
    "MG": ("2B", "5M", "T2",),
    "B1": ("4A", "2W", "4B", "1W",),
    "MM": ("5A",),
    "MF": (),
    "LN": ("5B", "4W",),
    "QN": ("3W", "5W",),
    "QF": (),
    "WO": (),
}


def on_device(
    tokens, w_qkv0, w_out0, gain0, bias0, rel0, shift, gain_merge, w_merge, gain1, w_qkv1,
    w_out1, bias1, rel1,
):
    vmem = pl.BlockSpec(memory_space=pltpu.VMEM)
    hbm = pl.BlockSpec(memory_space=pltpu.HBM)
    smem = pl.BlockSpec(memory_space=pltpu.SMEM)
    result = pl.pallas_call(
        kernel,
        out_shape=jax.ShapeDtypeStruct((64, 1024), BF16),
        in_specs=[smem] + [hbm] * 13,
        out_specs=vmem,
        scratch_shapes=[
            pltpu.VMEM((16, 16, 512), BF16),
            pltpu.VMEM((8, 192, 512), BF16),
            pltpu.VMEM((512, 512), BF16),
            pltpu.VMEM((1, 512), F32),
            pltpu.VMEM((64, 64), jnp.int32),
            pltpu.VMEM((8, 225), F32),
            pltpu.VMEM((1, 2048), F32),
            pltpu.VMEM((1, 1024), F32),
            pltpu.VMEM((1, 225), F32),
            pltpu.VMEM((64, 64), jnp.int32),
            pltpu.VMEM((8, 256), F32),
            pltpu.VMEM((32, 256), jnp.int32),
            pltpu.VMEM((576, 512), BF16),
            pltpu.VMEM((16, 64, 512), BF16),
            pltpu.VMEM((8, 128, 1024), BF16),
            pltpu.VMEM((8, 192, 1024), BF16),
            pltpu.VMEM((8, 64, 1024), BF16),
            pltpu.VMEM((8, 8, 256), F32),
            pltpu.VMEM((4, 64, 128), F32),
            pltpu.VMEM((4, 64, 128), F32),
            pltpu.VMEM((2, 8, 64, 128), BF16),
            pltpu.VMEM((8, 64, 128), BF16),
            pltpu.VMEM((128, 1024), BF16),
            pltpu.VMEM((128, 1024), BF16),
            pltpu.VMEM((64, 1024), BF16),
            pltpu.VMEM((64, 1024), BF16),
            pltpu.VMEM((64, 1024), BF16),
            pltpu.VMEM((192, 512), BF16),
            pltpu.SemaphoreType.DMA((COPIES,)),
            pltpu.SemaphoreType.DMA((COPIES,)),
            pltpu.SemaphoreType.DMA((13,)),
        ],
        compiler_params=pltpu.CompilerParams(
            collective_id=0, has_side_effects=True, vmem_limit_bytes=60 << 20
        ),
        name="swin",
    )(
        shift, tokens, w_qkv0, w_out0, gain0.reshape(1, 512), rel0, bias0,
        gain_merge.reshape(1, 2048), w_merge, gain1.reshape(1, 1024),
        w_qkv1.reshape(192, 1024), w_out1, bias1, rel1,
    )
    return result.reshape(8, 8, 1024)


def solution(mesh):
    placed = (
        P("lat", "lon", None),
        P(),
        P(),
        P(),
        P(),
        P(),
        P(),
        P(),
        P("lat", None),
        P(),
        P("lat", None, None),
        P("lat", None),
        P("lat", None),
        P(),
    )
    return jax.shard_map(
        on_device, mesh=mesh, in_specs=placed, out_specs=P("lat", "lon", None), check_vma=False
    )
```

```python
import functools

import jax
import jax.numpy as jnp
from jax import lax
from jax.experimental import pallas as pl
from jax.experimental.pallas import tpu as pltpu
from jax.sharding import PartitionSpec as P

WIN = 8
EPS = 1e-05
NEG = -1e30
MESH = pl.DeviceIdType.MESH
F32 = jnp.float32
BF16 = jnp.bfloat16


def place():
    lat = lax.axis_index("lat")
    lon = lax.axis_index("lon")
    x = lax.div(lat, 4)
    half = lax.rem(lax.div(lat, 2), 2)
    core = lax.rem(lat, 2)
    y = half * 4 + lax.div(lon, 8)
    z = lax.rem(lon, 8)
    return lat, lon, x, y, z, core


def at(x, y, z, core):
    return (
        lax.rem(x + 4, 4) * 4 + lax.div(y, 4) * 2 + core,
        lax.rem(y, 4) * 8 + lax.rem(z + 8, 8),
    )


def dot_nt(left, right):
    return lax.dot_general(left, right, (((1,), (1,)), ((), ())), preferred_element_type=F32)


def dot_nn(left, right):
    return jnp.dot(left, right, preferred_element_type=F32)


def norm_rows(values, gain):
    mean = jnp.mean(values, axis=-1, keepdims=True)
    centred = values - mean
    spread = jnp.mean(centred * centred, axis=-1, keepdims=True)
    return centred * lax.rsqrt(spread + EPS) * gain


def lane_masks():
    lane = lax.broadcasted_iota(jnp.int32, (64, 128), 1)
    return lane < 64


def attend_pair(q2, k2, v2, bias, mask):
    low = lane_masks()
    low_b = low.astype(F32).astype(BF16)
    high_b = (1.0 - low.astype(F32)).astype(BF16)
    keys = jnp.concatenate([k2 * low_b, k2 * high_b], axis=0)
    scores = dot_nt(q2, keys) + bias
    if mask is not None:
        scores = scores + mask
    peak_a = jnp.max(jnp.where(low, scores, -jnp.inf), axis=-1, keepdims=True)
    peak_b = jnp.max(jnp.where(low, -jnp.inf, scores), axis=-1, keepdims=True)
    weights = jnp.exp(scores - jnp.where(low, peak_a, peak_b)).astype(BF16)
    values = jnp.concatenate([v2 * low_b, v2 * high_b], axis=0)
    ones = jnp.concatenate([low_b, high_b], axis=0)
    mixed = dot_nn(weights, jnp.concatenate([values, ones], axis=1))
    return (mixed[:, :128] / mixed[:, 128:]).astype(BF16)


def fill_bias(table, rel, rel2, out):
    coarse_part = table.astype(BF16).astype(F32)
    split = jnp.concatenate([coarse_part, table - coarse_part], axis=0).astype(BF16)
    entry = lax.broadcasted_iota(jnp.int32, (256, 256), 0)
    low = lax.broadcasted_iota(jnp.int32, (1, 128), 1) < 64
    rel2[...] = jnp.concatenate([rel[:32], rel[:32], rel[32:], rel[32:]], axis=1)

    def step(p, carry):
        row = rel2[pl.ds(p, 1), :]
        onehot = jnp.where(entry == row, 1.0, 0.0).astype(BF16)
        found = dot_nn(split, onehot)
        found = found[:8] + found[8:]
        for side in range(2):
            cols = slice(128 * side, 128 * side + 128)
            for t in range(4):
                out[t, pl.ds(p + 32 * side, 1), :] = jnp.where(
                    low, found[2 * t : 2 * t + 1, cols], found[2 * t + 1 : 2 * t + 2, cols]
                )
        return carry

    lax.fori_loop(0, 32, step, 0, unroll=4)


def kernel(
    shift, tok_h, w0_h, wo0_h, g0_h, rel0_h, bias0_h, gm_h, wm, g1_h, wq, wo, bias1_h, rel1_h,
    out,
    tok, w0, wo0, g0, rel0, bias0, gm, g1, bias1, rel1, tab0, rel2,
    fine_ref, hq, wide_m, wide_q, wide_o, tabs, b0, b1, mg, mo,
    part_s, part_r, upd_s, upd_r, coarse_ref, attn, ss, rs, ls,
):
    loads = [
        pltpu.make_async_copy(src, dst, ls.at[n])
        for n, (src, dst) in enumerate([
            (tok_h, tok), (bias1_h, bias1), (bias0_h, bias0), (rel0_h, rel0), (g0_h, g0),
            (w0_h, w0), (wo0_h, wo0), (gm_h, gm), (g1_h, g1), (rel1_h, rel1),
            (wm, wide_m.at[0]), (wq, wide_q.at[0]), (wo, wide_o.at[0]),
        ])
    ]
    for copy in loads:
        copy.start()
    lat, lon, x, y, z, core = place()
    half = lax.div(y, 4)
    a = shift[0]
    b = shift[1]

    to_xp, to_xm, to_x2 = at(x + 1, y, z, core), at(x - 1, y, z, core), at(x + 2, y, z, core)
    to_mir = at(x, 7 - y, z, core)
    to_yp, to_ym = at(x, lax.rem(y + 1, 8), z, core), at(x, lax.rem(y + 7, 8), z, core)
    to_zp, to_zm = at(x, y, z + 1, core), at(x, y, z - 1, core)
    to_core = at(x, y, z, 1 - core)
    to_pair = at(x, y + 1 - 2 * lax.rem(y, 2), z, core)
    depth = lax.rem(y, 4)
    edge = (depth == 0) | (depth == 3)
    outward = jnp.where(depth < 2, 7, 1)
    to_out = at(x, lax.rem(y + outward, 8), z, core)
    to_in = at(x, lax.rem(y + 8 - outward, 8), z, core)
    to_out2 = at(x, lax.rem(y + 2 * outward, 8), z, core)
    to_y2, to_ym2 = at(x, lax.rem(y + 2, 8), z, core), at(x, lax.rem(y + 6, 8), z, core)
    near, far = lax.rem(lat + 1 + 14 * core, 16), lax.rem(lat + 15 + 2 * core, 16)
    left, right = lax.rem(lon + 31, 32), lax.rem(lon + 1, 32)

    barrier = pltpu.get_barrier_semaphore()
    partners = [
        to_xp, to_xm, to_x2, to_mir, to_yp, to_ym, to_zp, to_zm, to_core,
        (far, lon), (lat, left), (lat, right), to_y2, to_ym2,
    ]
    for dev in partners:
        pl.semaphore_signal(barrier, inc=1, device_id=dev, device_id_type=MESH)
    loads[0].wait()
    for i in range(2):
        for j in range(2):
            block = tok[8 * i : 8 * i + 8].astype(F32)[:, 8 * j : 8 * j + 8, :]
            hq[4 * i + j + 5] = block.reshape(64, 512).astype(BF16)
    loads[1].wait()
    tabs[0] = jnp.zeros((8, 256), F32)
    tabs[0, :, 0:225] = jnp.broadcast_to(bias1[...], (8, 225))
    pl.semaphore_wait(barrier, len(partners))

    made = []

    def remote(src, dst, dev, take=None):
        k = len(made)
        copy = pltpu.make_async_remote_copy(
            src_ref=src, dst_ref=dst, send_sem=ss.at[k],
            recv_sem=rs.at[k if take is None else take],
            device_id=dev, device_id_type=MESH,
        )
        made.append(copy)
        return copy

    def start_all(copies):
        for copy in copies:
            copy.start()

    def recv_all(copies):
        for copy in copies:
            copy.wait_recv()

    far_at = 1 + 12 * core
    halo_near = [remote(hq.at[pl.ds(9 - 4 * core, 2)], hq.at[pl.ds(1 + 12 * core, 2)], (near, lon))]
    halo_far = [remote(hq.at[pl.ds(5 + 4 * core, 2)], hq.at[pl.ds(13 - 12 * core, 2)], (far, lon))]
    halo_lon = [
        remote(hq.at[6], hq.at[4], (lat, right)),
        remote(hq.at[10], hq.at[8], (lat, right)),
        remote(hq.at[5], hq.at[7], (lat, left)),
        remote(hq.at[9], hq.at[11], (lat, left)),
    ]
    corner_near = [
        remote(hq.at[8 - 4 * core], hq.at[12 * core], (near, lon)),
        remote(hq.at[11 - 4 * core], hq.at[3 + 12 * core], (near, lon)),
    ]
    corner_far = [
        remote(hq.at[far_at + 1], hq.at[far_at - 1], (lat, right)),
        remote(hq.at[far_at], hq.at[far_at + 2], (lat, left)),
    ]
    start_all(halo_lon + halo_near + halo_far)

    parity = lax.rem(z, 2)
    tab_first = [
        remote(tabs.at[0], tabs.at[2], to_xp),
        remote(tabs.at[0], tabs.at[1], to_xm),
        remote(tabs.at[0], tabs.at[3], to_x2),
        remote(tabs.at[0], tabs.at[4], to_mir),
    ]
    tab_second = [
        remote(tabs.at[4], tabs.at[6], to_xp),
        remote(tabs.at[4], tabs.at[5], to_xm),
        remote(tabs.at[4], tabs.at[7], to_x2),
    ]

    class Piece:
        def __init__(self, src, wide, base, rows, name):
            whole, by_y, direct = name in WHOLE, name in BY_Y, name in DIRECT
            size = rows // 2

            def parts(by):
                start = pl.multiple_of(base + by * size, 16)
                return (
                    pl.ds(start, size),
                    pl.ds(start, size // 2),
                    pl.ds(pl.multiple_of(start + size // 2, 16), size // 2),
                )

            part, part_a, part_b = parts(parity)
            side, side_a, side_b = parts(lax.rem(depth, 2) if by_y else parity)
            first = pl.ds(base, rows) if whole else side

            def swap(slot, count):
                slots = pl.ds(slot, count)
                return [
                    remote(wide.at[slots, part_a], wide.at[slots, part_a], to_zp),
                    remote(wide.at[slots, part_b], wide.at[slots, part_b], to_zm),
                ]

            def swap_y(slot, count):
                slots = pl.ds(slot, count)
                return [remote(wide.at[slots, side], wide.at[slots, side], to_pair)]

            self.whole = whole
            self.side = [
                remote(src.at[first], wide.at[2, first], to_xp),
                remote(src.at[first], wide.at[1, first], to_xm),
            ]
            take = len(made)
            self.cross = remote(src.at[part], wide.at[4, part], to_out)
            self.direct = direct
            if direct:
                self.inward = remote(src.at[part], wide.at[4, part], to_out2, take)
            else:
                self.inward = remote(wide.at[4, part], wide.at[4, part], to_in, take)
            self.on = [
                remote(wide.at[2, side_a], wide.at[3, side_a], to_xp),
                remote(wide.at[1, side_b], wide.at[3, side_b], to_xm),
            ]
            self.far_side = [
                remote(wide.at[4, part], wide.at[6, part], to_xp),
                remote(wide.at[4, part], wide.at[5, part], to_xm),
            ]
            self.far_on = [
                remote(wide.at[6, part_a], wide.at[7, part_a], to_xp),
                remote(wide.at[5, part_b], wide.at[7, part_b], to_xm),
            ]
            if by_y:
                self.swaps = [[] if whole else swap_y(1, 2), swap_y(3, 1), swap(4, 3), swap(7, 1)]
            else:
                self.swaps = [[] if whole else swap(1, 2), swap(3, 2), swap(5, 2), swap(7, 1)]

        def step(self, n):
            if n == 0:
                start_all(self.side)
                pl.when(edge)(self.cross.start)
                if self.direct:
                    pl.when(edge)(self.inward.start)
            if n == 1:
                recv_all(self.side)
                start_all(self.on)
                start_all(self.swaps[0])
            if n == 2:
                self.cross.wait_recv()
                if not self.direct:
                    pl.when(edge)(self.inward.start)
                start_all(self.far_side)
            if n == 3:
                recv_all(self.on)
                start_all(self.swaps[1])
            if n == 4:
                recv_all(self.far_side)
                start_all(self.far_on)
                start_all(self.swaps[2])
            if n == 5:
                recv_all(self.far_on)
                start_all(self.swaps[3])

        def finish(self, near):
            for swap in self.swaps[:2] if near else self.swaps[2:]:
                recv_all(swap)

        def sent(self):
            @pl.when(edge)
            def _():
                self.cross.wait_send()
                self.inward.wait_send()

    pieces = {
        "M": Piece(wm, wide_m, 0, 128, "M"),
        "A": Piece(wq, wide_q, 0, 128, "A"),
        "B": Piece(wq, wide_q, 128, 64, "B"),
        "W": Piece(wo, wide_o, 0, 64, "W"),
    }

    def events(name):
        for event in EVENTS[name]:
            if event == "T1":
                start_all(tab_first)
            elif event == "T2":
                recv_all(tab_first)
                start_all(tab_second)
            elif event == "CF":
                recv_all(halo_far)
                start_all(corner_far)
            else:
                pieces[event[1]].step(int(event[0]))

    events("B0")

    want = lax.broadcasted_iota(jnp.int32, (192, 1), 0)
    want_r = a + ((want & 63) >> 3)
    want_c = b + 8 * (want >> 6) + (want & 7)
    want = (want_r >> 3) * 256 + (want_c >> 3) * 64 + (want_r & 7) * 8 + (want_c & 7)
    pick = lax.broadcasted_iota(jnp.int32, (192, 512), 1) == want
    pick = jnp.where(pick, 1.0, 0.0).astype(BF16)
    for copy in loads[2:]:
        copy.wait()
    tab0[...] = jnp.zeros((8, 256), F32)
    tab0[:, 0:225] = bias0[...]
    fill_bias(tab0[...], rel0[...], rel2, b0)

    def window_row(k, carry):
        i = jnp.where(k == 0, 1, jnp.where(k == 1, 2 - 2 * core, 2 * core))

        @pl.when(k == 0)
        def _():
            events("R0a")
            recv_all(halo_lon)
            start_all(corner_near)

        @pl.when(k == 1)
        def _():
            events("R1a")
            recv_all(halo_near)
            recv_all(corner_near)

        @pl.when(k == 2)
        def _():
            events("R2a")
            recv_all(corner_far)

        cells = dot_nn(pick, hq[pl.ds(4 * i, 8)].reshape(512, 512))
        normed = norm_rows(cells, g0[...]).astype(BF16)
        query = (dot_nt(normed, w0[:, 0:64, :].reshape(512, 512)) * 0.125).astype(BF16)
        keys = dot_nt(normed, w0[:, 64:128, :].reshape(512, 512)).astype(BF16)
        values = dot_nt(normed, w0[:, 128:192, :].reshape(512, 512)).astype(BF16)
        for n in range(3):
            pl.when(k == n)(functools.partial(events, "R%db" % n))
        lane = lax.broadcasted_iota(jnp.int32, (1, 128), 1)
        row = lat * 16 + a - 8 + 8 * i + ((lane & 63) >> 3)
        mask = jnp.where((row >= 0) & (row < 256), 0.0, NEG)
        for w in range(3):
            rows = slice(64 * w, 64 * w + 64)
            for t in range(4):
                cols = slice(128 * t, 128 * t + 128)
                attn[rows, cols] = attend_pair(
                    query[rows, cols], keys[rows, cols], values[rows, cols], b0[t], mask
                )
        fine = cells + dot_nn(attn[...], wo0[...])
        fine_ref[pl.ds(pl.multiple_of(192 * i, 64), 192), :] = fine.astype(BF16)
        return carry

    lax.fori_loop(0, 3, window_row, 0)
    events("MG")

    want = lax.broadcasted_iota(jnp.int32, (256, 1), 0)
    want_r = 8 - a + 2 * ((want >> 3) & 7) + (want >> 7)
    want_c = 8 - b + 2 * (want & 7) + ((want >> 6) & 1)
    want = (want_r >> 3) * 192 + (want_c >> 3) * 64 + (want_r & 7) * 8 + (want_c & 7)
    pick = lax.broadcasted_iota(jnp.int32, (256, 576), 1) == want
    pick = jnp.where(pick, 1.0, 0.0).astype(BF16)
    picked = dot_nn(pick, fine_ref[...])
    blocks = [picked[64 * k : 64 * k + 64] for k in range(4)]
    total = sum(jnp.sum(block, axis=-1, keepdims=True) for block in blocks)
    mean = total * (1.0 / 2048)
    blocks = [block - mean for block in blocks]
    spread = sum(jnp.sum(block * block, axis=-1, keepdims=True) for block in blocks)
    scale = lax.rsqrt(spread * (1.0 / 2048) + EPS)
    for k in range(4):
        merged = (blocks[k] * scale * gm[:, 512 * k : 512 * k + 512]).astype(BF16)
        for m in range(4):
            chunk = 4 * k + m
            mg[chunk % 2, chunk // 2] = merged[:, 128 * m : 128 * m + 128]

    give_merged = remote(mg.at[1 - core], mo, to_core)
    give_part = remote(part_s, part_r, to_core)
    give_upd = remote(upd_s, upd_r, to_core)
    give_merged.start()
    events("B1")
    recv_all(tab_second)
    sub = lax.broadcasted_iota(jnp.int32, (8, 256), 0)
    table = jnp.zeros((8, 256), F32)
    for n, slot in enumerate(range(8)):
        table = jnp.where(sub == n, tabs[slot], table)
    fill_bias(table, rel1[...], rel2, b1)

    give_merged.wait_recv()
    slots = [
        2 * lax.rem(x + step, 4) + side for side in (half, 1 - half) for step in (0, 1, 3, 2)
    ]
    mine = jnp.concatenate([mg[core, slot] for slot in slots], axis=1)
    theirs = jnp.concatenate([mo[slot] for slot in slots], axis=1)
    merged = jnp.concatenate([theirs, mine], axis=0)
    events("MM")
    pieces["M"].finish(True)
    partial = dot_nn(merged[:, :512], wide_m[0:4].reshape(512, 1024))
    events("MF")
    pieces["M"].finish(False)
    partial = partial + dot_nn(merged[:, 512:], wide_m[4:8].reshape(512, 1024))
    part_s[...] = partial.astype(BF16)
    give_part.start()
    events("LN")
    give_part.wait_recv()
    coarse = (partial[64:] + part_r[0:64].astype(F32)).astype(BF16)
    coarse_ref[...] = coarse
    others = (partial[:64] + part_r[64:128].astype(F32)).astype(BF16)
    both = jnp.concatenate([coarse, others], axis=0).astype(F32)
    normed = norm_rows(both, g1[...]).astype(BF16)
    for g in range(2):
        events("QN" if g == 0 else "QF")
        pieces["A"].finish(g == 0)
        pieces["B"].finish(g == 0)
        heads = slice(4 * g, 4 * g + 4)
        query = dot_nt(normed, wide_q[heads, 0:64, :].reshape(256, 1024)) * 0.125
        query = query.astype(BF16)
        keys = dot_nt(normed, wide_q[heads, 64:128, :].reshape(256, 1024)).astype(BF16)
        values = dot_nt(normed, wide_q[heads, 128:192, :].reshape(256, 1024)).astype(BF16)
        for w in range(2):
            rows = slice(64 * w, 64 * w + 64)
            for t in range(2):
                cols = slice(128 * t, 128 * t + 128)
                pair = 2 * g + t
                attn[rows, 128 * pair : 128 * pair + 128] = attend_pair(
                    query[rows, cols], keys[rows, cols], values[rows, cols], b1[pair], None
                )
    events("WO")
    pieces["W"].finish(True)
    pieces["W"].finish(False)
    w_out = wide_o[...].reshape(512, 1024)
    upd_s[...] = dot_nn(attn[64:128, :], w_out).astype(BF16)
    give_upd.start()
    update = coarse_ref[...].astype(F32) + dot_nn(attn[0:64, :], w_out)
    give_upd.wait_recv()
    out[...] = (update + upd_r[...].astype(F32)).astype(BF16).reshape(8, 8, 1024)
    for piece in pieces.values():
        piece.sent()
    conditional = [c for piece in pieces.values() for c in (piece.cross, piece.inward)]
    for copy in made:
        if not any(copy is c for c in conditional):
            copy.wait_send()


COPIES = 10 + 7 + 4 * 18 + 3
WHOLE = "BW"
BY_Y = "ABW"
DIRECT = "ABMW"
EVENTS = {
    "B0": ("T1", "0M", "0B",),
    "R0a": ("1M", "0A", "1B", "0W",),
    "R0b": (),
    "R1a": ("2M", "CF", "3M",),
    "R1b": ("2B", "1A", "3B",),
    "R2a": ("4M", "4B", "1W",),
    "R2b": ("3A", "2A",),
    "MG": ("5M", "5B", "2W", "T2",),
    "B1": ("4A",),
    "MM": (),
    "MF": ("3W",),
    "LN": ("5A", "4W",),
    "QN": ("5W",),
    "QF": (),
    "WO": (),
}


def on_device(
    tokens, w_qkv0, w_out0, gain0, bias0, rel0, shift, gain_merge, w_merge, gain1, w_qkv1,
    w_out1, bias1, rel1,
):
    vmem = pl.BlockSpec(memory_space=pltpu.VMEM)
    hbm = pl.BlockSpec(memory_space=pltpu.HBM)
    smem = pl.BlockSpec(memory_space=pltpu.SMEM)
    result = pl.pallas_call(
        kernel,
        out_shape=jax.ShapeDtypeStruct((8, 8, 1024), BF16),
        in_specs=[smem] + [hbm] * 13,
        out_specs=vmem,
        scratch_shapes=[
            pltpu.VMEM((16, 16, 512), BF16),
            pltpu.VMEM((8, 192, 512), BF16),
            pltpu.VMEM((512, 512), BF16),
            pltpu.VMEM((1, 512), F32),
            pltpu.VMEM((64, 64), jnp.int32),
            pltpu.VMEM((8, 225), F32),
            pltpu.VMEM((1, 2048), F32),
            pltpu.VMEM((1, 1024), F32),
            pltpu.VMEM((1, 225), F32),
            pltpu.VMEM((64, 64), jnp.int32),
            pltpu.VMEM((8, 256), F32),
            pltpu.VMEM((32, 256), jnp.int32),
            pltpu.VMEM((576, 512), BF16),
            pltpu.VMEM((16, 64, 512), BF16),
            pltpu.VMEM((8, 128, 1024), BF16),
            pltpu.VMEM((8, 192, 1024), BF16),
            pltpu.VMEM((8, 64, 1024), BF16),
            pltpu.VMEM((8, 8, 256), F32),
            pltpu.VMEM((4, 64, 128), F32),
            pltpu.VMEM((4, 64, 128), F32),
            pltpu.VMEM((2, 8, 64, 128), BF16),
            pltpu.VMEM((8, 64, 128), BF16),
            pltpu.VMEM((128, 1024), BF16),
            pltpu.VMEM((128, 1024), BF16),
            pltpu.VMEM((64, 1024), BF16),
            pltpu.VMEM((64, 1024), BF16),
            pltpu.VMEM((64, 1024), BF16),
            pltpu.VMEM((192, 512), BF16),
            pltpu.SemaphoreType.DMA((COPIES,)),
            pltpu.SemaphoreType.DMA((COPIES,)),
            pltpu.SemaphoreType.DMA((13,)),
        ],
        compiler_params=pltpu.CompilerParams(
            collective_id=0, has_side_effects=True, vmem_limit_bytes=60 << 20
        ),
        name="swin",
    )(
        shift, tokens, w_qkv0, w_out0, gain0.reshape(1, 512), rel0, bias0,
        gain_merge.reshape(1, 2048), w_merge, gain1.reshape(1, 1024),
        w_qkv1.reshape(192, 1024), w_out1, bias1, rel1,
    )
    return result


def solution(mesh):
    placed = (
        P("lat", "lon", None),
        P(),
        P(),
        P(),
        P(),
        P(),
        P(),
        P(),
        P("lat", None),
        P(),
        P("lat", None, None),
        P("lat", None),
        P("lat", None),
        P(),
    )
    return jax.shard_map(
        on_device, mesh=mesh, in_specs=placed, out_specs=P("lat", "lon", None), check_vma=False
    )
```

```python
import functools

import jax
import jax.numpy as jnp
from jax import lax
from jax.experimental import pallas as pl
from jax.experimental.pallas import tpu as pltpu
from jax.sharding import PartitionSpec as P

WIN = 8
EPS = 1e-05
NEG = -1e30
MESH = pl.DeviceIdType.MESH
F32 = jnp.float32
BF16 = jnp.bfloat16


def place():
    lat = lax.axis_index("lat")
    lon = lax.axis_index("lon")
    x = lax.div(lat, 4)
    half = lax.rem(lax.div(lat, 2), 2)
    core = lax.rem(lat, 2)
    y = half * 4 + lax.div(lon, 8)
    z = lax.rem(lon, 8)
    return lat, lon, x, y, z, core


def at(x, y, z, core):
    return (
        lax.rem(x + 4, 4) * 4 + lax.div(y, 4) * 2 + core,
        lax.rem(y, 4) * 8 + lax.rem(z + 8, 8),
    )


def dot_nt(left, right):
    return lax.dot_general(left, right, (((1,), (1,)), ((), ())), preferred_element_type=F32)


def dot_nn(left, right):
    return jnp.dot(left, right, preferred_element_type=F32)


def norm_rows(values, gain):
    mean = jnp.mean(values, axis=-1, keepdims=True)
    centred = values - mean
    spread = jnp.mean(centred * centred, axis=-1, keepdims=True)
    return centred * lax.rsqrt(spread + EPS) * gain


def lane_masks():
    lane = lax.broadcasted_iota(jnp.int32, (64, 128), 1)
    return lane < 64


def attend_pair(q2, k2, v2, bias, mask):
    low = lane_masks()
    low_b = low.astype(F32).astype(BF16)
    high_b = (1.0 - low.astype(F32)).astype(BF16)
    keys = jnp.concatenate([k2 * low_b, k2 * high_b], axis=0)
    scores = dot_nt(q2, keys) + bias
    if mask is not None:
        scores = scores + mask
    peak_a = jnp.max(jnp.where(low, scores, -jnp.inf), axis=-1, keepdims=True)
    peak_b = jnp.max(jnp.where(low, -jnp.inf, scores), axis=-1, keepdims=True)
    weights = jnp.exp(scores - jnp.where(low, peak_a, peak_b)).astype(BF16)
    values = jnp.concatenate([v2 * low_b, v2 * high_b], axis=0)
    ones = jnp.concatenate([low_b, high_b], axis=0)
    mixed = dot_nn(weights, jnp.concatenate([values, ones], axis=1))
    return (mixed[:, :128] / mixed[:, 128:]).astype(BF16)


def fill_bias(table, rel, rel2, out):
    coarse_part = table.astype(BF16).astype(F32)
    split = jnp.concatenate([coarse_part, table - coarse_part], axis=0).astype(BF16)
    entry = lax.broadcasted_iota(jnp.int32, (256, 256), 0)
    low = lax.broadcasted_iota(jnp.int32, (1, 128), 1) < 64
    rel2[...] = jnp.concatenate([rel[:32], rel[:32], rel[32:], rel[32:]], axis=1)

    def step(p, carry):
        row = rel2[pl.ds(p, 1), :]
        onehot = jnp.where(entry == row, 1.0, 0.0).astype(BF16)
        found = dot_nn(split, onehot)
        found = found[:8] + found[8:]
        for side in range(2):
            cols = slice(128 * side, 128 * side + 128)
            for t in range(4):
                out[t, pl.ds(p + 32 * side, 1), :] = jnp.where(
                    low, found[2 * t : 2 * t + 1, cols], found[2 * t + 1 : 2 * t + 2, cols]
                )
        return carry

    lax.fori_loop(0, 32, step, 0, unroll=4)


def kernel(
    shift, tok_h, w0_h, wo0_h, g0_h, rel0_h, bias0_h, gm_h, wm, g1_h, wq, wo, bias1_h, rel1_h,
    out,
    tok, w0, wo0, g0, rel0, bias0, gm, g1, bias1, rel1, tab0, rel2,
    fine_ref, hq, wide_m, wide_q, wide_o, tabs, b0, b1, mg, mo,
    part_s, part_r, upd_s, upd_r, coarse_ref, attn, ss, rs, ls,
):
    loads = [
        pltpu.make_async_copy(src, dst, ls.at[n])
        for n, (src, dst) in enumerate([
            (tok_h, tok), (bias1_h, bias1), (bias0_h, bias0), (rel0_h, rel0), (g0_h, g0),
            (w0_h, w0), (wo0_h, wo0), (gm_h, gm), (g1_h, g1), (rel1_h, rel1),
            (wm, wide_m.at[0]), (wq, wide_q.at[0]), (wo, wide_o.at[0]),
        ])
    ]
    for copy in loads:
        copy.start()
    lat, lon, x, y, z, core = place()
    half = lax.div(y, 4)
    a = shift[0]
    b = shift[1]

    to_xp, to_xm, to_x2 = at(x + 1, y, z, core), at(x - 1, y, z, core), at(x + 2, y, z, core)
    to_mir = at(x, 7 - y, z, core)
    to_yp, to_ym = at(x, lax.rem(y + 1, 8), z, core), at(x, lax.rem(y + 7, 8), z, core)
    to_zp, to_zm = at(x, y, z + 1, core), at(x, y, z - 1, core)
    to_core = at(x, y, z, 1 - core)
    to_pair = at(x, y + 1 - 2 * lax.rem(y, 2), z, core)
    depth = lax.rem(y, 4)
    edge = (depth == 0) | (depth == 3)
    outward = jnp.where(depth < 2, 7, 1)
    to_out = at(x, lax.rem(y + outward, 8), z, core)
    to_in = at(x, lax.rem(y + 8 - outward, 8), z, core)
    to_out2 = at(x, lax.rem(y + 2 * outward, 8), z, core)
    to_y2, to_ym2 = at(x, lax.rem(y + 2, 8), z, core), at(x, lax.rem(y + 6, 8), z, core)
    near, far = lax.rem(lat + 1 + 14 * core, 16), lax.rem(lat + 15 + 2 * core, 16)
    left, right = lax.rem(lon + 31, 32), lax.rem(lon + 1, 32)

    barrier = pltpu.get_barrier_semaphore()
    partners = [
        to_xp, to_xm, to_x2, to_mir, to_yp, to_ym, to_zp, to_zm, to_core,
        (far, lon), (lat, left), (lat, right), to_y2, to_ym2,
    ]
    for dev in partners:
        pl.semaphore_signal(barrier, inc=1, device_id=dev, device_id_type=MESH)
    loads[0].wait()
    for i in range(2):
        for j in range(2):
            block = tok[8 * i : 8 * i + 8].astype(F32)[:, 8 * j : 8 * j + 8, :]
            hq[4 * i + j + 5] = block.reshape(64, 512).astype(BF16)
    loads[1].wait()
    tabs[0] = jnp.zeros((8, 256), F32)
    tabs[0, :, 0:225] = jnp.broadcast_to(bias1[...], (8, 225))
    pl.semaphore_wait(barrier, len(partners))

    made = []

    def remote(src, dst, dev, take=None):
        k = len(made)
        copy = pltpu.make_async_remote_copy(
            src_ref=src, dst_ref=dst, send_sem=ss.at[k],
            recv_sem=rs.at[k if take is None else take],
            device_id=dev, device_id_type=MESH,
        )
        made.append(copy)
        return copy

    def start_all(copies):
        for copy in copies:
            copy.start()

    def recv_all(copies):
        for copy in copies:
            copy.wait_recv()

    far_at = 1 + 12 * core
    halo_near = [remote(hq.at[pl.ds(9 - 4 * core, 2)], hq.at[pl.ds(1 + 12 * core, 2)], (near, lon))]
    halo_far = [remote(hq.at[pl.ds(5 + 4 * core, 2)], hq.at[pl.ds(13 - 12 * core, 2)], (far, lon))]
    halo_lon = [
        remote(hq.at[6], hq.at[4], (lat, right)),
        remote(hq.at[10], hq.at[8], (lat, right)),
        remote(hq.at[5], hq.at[7], (lat, left)),
        remote(hq.at[9], hq.at[11], (lat, left)),
    ]
    corner_near = [
        remote(hq.at[8 - 4 * core], hq.at[12 * core], (near, lon)),
        remote(hq.at[11 - 4 * core], hq.at[3 + 12 * core], (near, lon)),
    ]
    corner_far = [
        remote(hq.at[far_at + 1], hq.at[far_at - 1], (lat, right)),
        remote(hq.at[far_at], hq.at[far_at + 2], (lat, left)),
    ]
    start_all(halo_lon + halo_near + halo_far)

    parity = lax.rem(z, 2)
    tab_first = [
        remote(tabs.at[0], tabs.at[2], to_xp),
        remote(tabs.at[0], tabs.at[1], to_xm),
        remote(tabs.at[0], tabs.at[3], to_x2),
        remote(tabs.at[0], tabs.at[4], to_mir),
    ]
    tab_second = [
        remote(tabs.at[4], tabs.at[6], to_xp),
        remote(tabs.at[4], tabs.at[5], to_xm),
        remote(tabs.at[4], tabs.at[7], to_x2),
    ]

    class Piece:
        def __init__(self, src, wide, base, rows, name):
            whole, by_y, direct = name in WHOLE, name in BY_Y, name in DIRECT
            size = rows // 2

            def parts(by):
                start = pl.multiple_of(base + by * size, 16)
                return (
                    pl.ds(start, size),
                    pl.ds(start, size // 2),
                    pl.ds(pl.multiple_of(start + size // 2, 16), size // 2),
                )

            part, part_a, part_b = parts(parity)
            side, side_a, side_b = parts(lax.rem(depth, 2) if by_y else parity)
            first = pl.ds(base, rows) if whole else side

            def swap(slot, count):
                slots = pl.ds(slot, count)
                return [
                    remote(wide.at[slots, part_a], wide.at[slots, part_a], to_zp),
                    remote(wide.at[slots, part_b], wide.at[slots, part_b], to_zm),
                ]

            def swap_y(slot, count):
                slots = pl.ds(slot, count)
                return [remote(wide.at[slots, side], wide.at[slots, side], to_pair)]

            self.whole = whole
            self.side = [
                remote(src.at[first], wide.at[2, first], to_xp),
                remote(src.at[first], wide.at[1, first], to_xm),
            ]
            take = len(made)
            self.cross = remote(src.at[part], wide.at[4, part], to_out)
            self.direct = direct
            if direct:
                self.inward = remote(src.at[part], wide.at[4, part], to_out2, take)
            else:
                self.inward = remote(wide.at[4, part], wide.at[4, part], to_in, take)
            self.on = [
                remote(wide.at[2, side_a], wide.at[3, side_a], to_xp),
                remote(wide.at[1, side_b], wide.at[3, side_b], to_xm),
            ]
            self.far_side = [
                remote(wide.at[4, part], wide.at[6, part], to_xp),
                remote(wide.at[4, part], wide.at[5, part], to_xm),
            ]
            self.far_on = [
                remote(wide.at[6, part_a], wide.at[7, part_a], to_xp),
                remote(wide.at[5, part_b], wide.at[7, part_b], to_xm),
            ]
            if by_y:
                self.swaps = [[] if whole else swap_y(1, 2), swap_y(3, 1), swap(4, 3), swap(7, 1)]
            else:
                self.swaps = [[] if whole else swap(1, 2), swap(3, 2), swap(5, 2), swap(7, 1)]

        def step(self, n):
            if n == 0:
                start_all(self.side)
                pl.when(edge)(self.cross.start)
                if self.direct:
                    pl.when(edge)(self.inward.start)
            if n == 1:
                recv_all(self.side)
                start_all(self.on)
                start_all(self.swaps[0])
            if n == 2:
                self.cross.wait_recv()
                if not self.direct:
                    pl.when(edge)(self.inward.start)
                start_all(self.far_side)
            if n == 3:
                recv_all(self.on)
                start_all(self.swaps[1])
            if n == 4:
                recv_all(self.far_side)
                start_all(self.far_on)
                start_all(self.swaps[2])
            if n == 5:
                recv_all(self.far_on)
                start_all(self.swaps[3])

        def finish(self, near):
            for swap in self.swaps[:2] if near else self.swaps[2:]:
                recv_all(swap)

        def sent(self):
            @pl.when(edge)
            def _():
                self.cross.wait_send()
                self.inward.wait_send()

    pieces = {
        "M": Piece(wm, wide_m, 0, 128, "M"),
        "A": Piece(wq, wide_q, 0, 128, "A"),
        "B": Piece(wq, wide_q, 128, 64, "B"),
        "W": Piece(wo, wide_o, 0, 64, "W"),
    }

    def events(name):
        for event in EVENTS[name]:
            if event == "T1":
                start_all(tab_first)
            elif event == "T2":
                recv_all(tab_first)
                start_all(tab_second)
            elif event == "CF":
                recv_all(halo_far)
                start_all(corner_far)
            else:
                pieces[event[1]].step(int(event[0]))

    events("B0")

    want = lax.broadcasted_iota(jnp.int32, (192, 1), 0)
    want_r = a + ((want & 63) >> 3)
    want_c = b + 8 * (want >> 6) + (want & 7)
    want = (want_r >> 3) * 256 + (want_c >> 3) * 64 + (want_r & 7) * 8 + (want_c & 7)
    pick = lax.broadcasted_iota(jnp.int32, (192, 512), 1) == want
    pick = jnp.where(pick, 1.0, 0.0).astype(BF16)
    for copy in loads[2:]:
        copy.wait()
    tab0[...] = jnp.zeros((8, 256), F32)
    tab0[:, 0:225] = bias0[...]
    fill_bias(tab0[...], rel0[...], rel2, b0)

    def window_row(k, carry):
        i = jnp.where(k == 0, 1, jnp.where(k == 1, 2 - 2 * core, 2 * core))

        @pl.when(k == 0)
        def _():
            events("R0a")
            recv_all(halo_lon)
            start_all(corner_near)

        @pl.when(k == 1)
        def _():
            events("R1a")
            recv_all(halo_near)
            recv_all(corner_near)

        @pl.when(k == 2)
        def _():
            events("R2a")
            recv_all(corner_far)

        cells = dot_nn(pick, hq[pl.ds(4 * i, 8)].reshape(512, 512))
        normed = norm_rows(cells, g0[...]).astype(BF16)
        query = (dot_nt(normed, w0[:, 0:64, :].reshape(512, 512)) * 0.125).astype(BF16)
        keys = dot_nt(normed, w0[:, 64:128, :].reshape(512, 512)).astype(BF16)
        values = dot_nt(normed, w0[:, 128:192, :].reshape(512, 512)).astype(BF16)
        for n in range(3):
            pl.when(k == n)(functools.partial(events, "R%db" % n))
        lane = lax.broadcasted_iota(jnp.int32, (1, 128), 1)
        row = lat * 16 + a - 8 + 8 * i + ((lane & 63) >> 3)
        mask = jnp.where((row >= 0) & (row < 256), 0.0, NEG)
        for w in range(3):
            rows = slice(64 * w, 64 * w + 64)
            for t in range(4):
                cols = slice(128 * t, 128 * t + 128)
                attn[rows, cols] = attend_pair(
                    query[rows, cols], keys[rows, cols], values[rows, cols], b0[t], mask
                )
        fine = cells + dot_nn(attn[...], wo0[...])
        fine_ref[pl.ds(pl.multiple_of(192 * i, 64), 192), :] = fine.astype(BF16)
        return carry

    lax.fori_loop(0, 3, window_row, 0)
    events("MG")

    want = lax.broadcasted_iota(jnp.int32, (256, 1), 0)
    want_r = 8 - a + 2 * ((want >> 3) & 7) + (want >> 7)
    want_c = 8 - b + 2 * (want & 7) + ((want >> 6) & 1)
    want = (want_r >> 3) * 192 + (want_c >> 3) * 64 + (want_r & 7) * 8 + (want_c & 7)
    pick = lax.broadcasted_iota(jnp.int32, (256, 576), 1) == want
    pick = jnp.where(pick, 1.0, 0.0).astype(BF16)
    picked = dot_nn(pick, fine_ref[...])
    blocks = [picked[64 * k : 64 * k + 64] for k in range(4)]
    total = sum(jnp.sum(block, axis=-1, keepdims=True) for block in blocks)
    mean = total * (1.0 / 2048)
    blocks = [block - mean for block in blocks]
    spread = sum(jnp.sum(block * block, axis=-1, keepdims=True) for block in blocks)
    scale = lax.rsqrt(spread * (1.0 / 2048) + EPS)
    for k in range(4):
        merged = (blocks[k] * scale * gm[:, 512 * k : 512 * k + 512]).astype(BF16)
        for m in range(4):
            chunk = 4 * k + m
            mg[chunk % 2, chunk // 2] = merged[:, 128 * m : 128 * m + 128]

    give_merged = remote(mg.at[1 - core], mo, to_core)
    give_part = remote(part_s, part_r, to_core)
    give_upd = remote(upd_s, upd_r, to_core)
    give_merged.start()
    events("B1")
    recv_all(tab_second)
    sub = lax.broadcasted_iota(jnp.int32, (8, 256), 0)
    table = jnp.zeros((8, 256), F32)
    for n, slot in enumerate(range(8)):
        table = jnp.where(sub == n, tabs[slot], table)
    fill_bias(table, rel1[...], rel2, b1)

    give_merged.wait_recv()
    slots = [
        2 * lax.rem(x + step, 4) + side for side in (half, 1 - half) for step in (0, 1, 3, 2)
    ]
    mine = jnp.concatenate([mg[core, slot] for slot in slots], axis=1)
    theirs = jnp.concatenate([mo[slot] for slot in slots], axis=1)
    merged = jnp.concatenate([theirs, mine], axis=0)
    events("MM")
    pieces["M"].finish(True)
    partial = dot_nn(merged[:, :512], wide_m[0:4].reshape(512, 1024))
    events("MF")
    pieces["M"].finish(False)
    partial = partial + dot_nn(merged[:, 512:], wide_m[4:8].reshape(512, 1024))
    part_s[...] = partial.astype(BF16)
    give_part.start()
    events("LN")
    give_part.wait_recv()
    coarse = (partial[64:] + part_r[0:64].astype(F32)).astype(BF16)
    coarse_ref[...] = coarse
    others = (partial[:64] + part_r[64:128].astype(F32)).astype(BF16)
    both = jnp.concatenate([coarse, others], axis=0).astype(F32)
    normed = norm_rows(both, g1[...]).astype(BF16)
    for g in range(2):
        events("QN" if g == 0 else "QF")
        pieces["A"].finish(g == 0)
        pieces["B"].finish(g == 0)
        heads = slice(4 * g, 4 * g + 4)
        query = dot_nt(normed, wide_q[heads, 0:64, :].reshape(256, 1024)) * 0.125
        query = query.astype(BF16)
        keys = dot_nt(normed, wide_q[heads, 64:128, :].reshape(256, 1024)).astype(BF16)
        values = dot_nt(normed, wide_q[heads, 128:192, :].reshape(256, 1024)).astype(BF16)
        for w in range(2):
            rows = slice(64 * w, 64 * w + 64)
            for t in range(2):
                cols = slice(128 * t, 128 * t + 128)
                pair = 2 * g + t
                attn[rows, 128 * pair : 128 * pair + 128] = attend_pair(
                    query[rows, cols], keys[rows, cols], values[rows, cols], b1[pair], None
                )
    events("WO")
    pieces["W"].finish(True)
    pieces["W"].finish(False)
    w_out = wide_o[...].reshape(512, 1024)
    upd_s[...] = dot_nn(attn[64:128, :], w_out).astype(BF16)
    give_upd.start()
    update = coarse_ref[...].astype(F32) + dot_nn(attn[0:64, :], w_out)
    give_upd.wait_recv()
    out[...] = (update + upd_r[...].astype(F32)).astype(BF16).reshape(8, 8, 1024)
    for piece in pieces.values():
        piece.sent()
    conditional = [c for piece in pieces.values() for c in (piece.cross, piece.inward)]
    for copy in made:
        if not any(copy is c for c in conditional):
            copy.wait_send()


COPIES = 10 + 7 + 4 * 18 + 3
WHOLE = ""
BY_Y = "ABW"
DIRECT = "ABMW"
EVENTS = {
    "B0": ("T1", "0M", "0B",),
    "R0a": ("1M", "0A", "1B", "0W",),
    "R0b": (),
    "R1a": ("2M", "CF", "3M",),
    "R1b": ("2B", "1A", "3B",),
    "R2a": ("4M", "4B", "1W",),
    "R2b": ("3A", "2A",),
    "MG": ("5M", "5B", "2W", "T2",),
    "B1": ("4A",),
    "MM": (),
    "MF": ("3W",),
    "LN": ("5A", "4W",),
    "QN": ("5W",),
    "QF": (),
    "WO": (),
}


def on_device(
    tokens, w_qkv0, w_out0, gain0, bias0, rel0, shift, gain_merge, w_merge, gain1, w_qkv1,
    w_out1, bias1, rel1,
):
    vmem = pl.BlockSpec(memory_space=pltpu.VMEM)
    hbm = pl.BlockSpec(memory_space=pltpu.HBM)
    smem = pl.BlockSpec(memory_space=pltpu.SMEM)
    result = pl.pallas_call(
        kernel,
        out_shape=jax.ShapeDtypeStruct((8, 8, 1024), BF16),
        in_specs=[smem] + [hbm] * 13,
        out_specs=vmem,
        scratch_shapes=[
            pltpu.VMEM((16, 16, 512), BF16),
            pltpu.VMEM((8, 192, 512), BF16),
            pltpu.VMEM((512, 512), BF16),
            pltpu.VMEM((1, 512), F32),
            pltpu.VMEM((64, 64), jnp.int32),
            pltpu.VMEM((8, 225), F32),
            pltpu.VMEM((1, 2048), F32),
            pltpu.VMEM((1, 1024), F32),
            pltpu.VMEM((1, 225), F32),
            pltpu.VMEM((64, 64), jnp.int32),
            pltpu.VMEM((8, 256), F32),
            pltpu.VMEM((32, 256), jnp.int32),
            pltpu.VMEM((576, 512), BF16),
            pltpu.VMEM((16, 64, 512), BF16),
            pltpu.VMEM((8, 128, 1024), BF16),
            pltpu.VMEM((8, 192, 1024), BF16),
            pltpu.VMEM((8, 64, 1024), BF16),
            pltpu.VMEM((8, 8, 256), F32),
            pltpu.VMEM((4, 64, 128), F32),
            pltpu.VMEM((4, 64, 128), F32),
            pltpu.VMEM((2, 8, 64, 128), BF16),
            pltpu.VMEM((8, 64, 128), BF16),
            pltpu.VMEM((128, 1024), BF16),
            pltpu.VMEM((128, 1024), BF16),
            pltpu.VMEM((64, 1024), BF16),
            pltpu.VMEM((64, 1024), BF16),
            pltpu.VMEM((64, 1024), BF16),
            pltpu.VMEM((192, 512), BF16),
            pltpu.SemaphoreType.DMA((COPIES,)),
            pltpu.SemaphoreType.DMA((COPIES,)),
            pltpu.SemaphoreType.DMA((13,)),
        ],
        compiler_params=pltpu.CompilerParams(
            collective_id=0, has_side_effects=True, vmem_limit_bytes=60 << 20
        ),
        name="swin",
    )(
        shift, tokens, w_qkv0, w_out0, gain0.reshape(1, 512), rel0, bias0,
        gain_merge.reshape(1, 2048), w_merge, gain1.reshape(1, 1024),
        w_qkv1.reshape(192, 1024), w_out1, bias1, rel1,
    )
    return result


def solution(mesh):
    placed = (
        P("lat", "lon", None),
        P(),
        P(),
        P(),
        P(),
        P(),
        P(),
        P(),
        P("lat", None),
        P(),
        P("lat", None, None),
        P("lat", None),
        P("lat", None),
        P(),
    )
    return jax.shard_map(
        on_device, mesh=mesh, in_specs=placed, out_specs=P("lat", "lon", None), check_vma=False
    )
```
